32 devices in a mesh: seq: 4 (over z), hid: 8 (over y, x, core).
Axes of the slice: x: 2, y: 2, z: 4, core: 2. Of those that a mesh axis runs over, the one named last changes fastest.
Arguments:
- tokens: bfloat16 [2048, 4, 2048], P(('seq', 'hid')), may hold values from -6 to 6
- lengths: int32 [4], replicated, may hold values from 512 to 2048, as said below
- cotangent: bfloat16 [2048, 4, 2048], P(('seq', 'hid')), may hold values from -6 to 6
- mixer_gain: float32 [2048], replicated, may hold values from 0.25 to 1.75
- query_weight: bfloat16 [2048, 2048], P(None, 'hid'), may hold values from -0.125 to 0.125
- forget_weight: bfloat16 [2048, 2048], P(None, 'hid'), may hold values from -0.125 to 0.125
- input_weight: bfloat16 [2048, 2048], P(None, 'hid'), may hold values from -0.125 to 0.125
- gate_weight: bfloat16 [2048, 2048], P(None, 'hid'), may hold values from -0.125 to 0.125
- lower_bound: float32 [2048], P('hid'), may hold values from 0.5 to 0.9995
- head_gain: float32 [2048], P('hid'), may hold values from 0.25 to 1.75
- out_weight: bfloat16 [2048, 2048], replicated, may hold values from -0.125 to 0.125
- feed_gain: float32 [2048], replicated, may hold values from 0.25 to 1.75
- feed_gate_weight: bfloat16 [2048, 5632], P(None, 'hid'), may hold values from -0.125 to 0.125
- up_weight: bfloat16 [2048, 5632], P(None, 'hid'), may hold values from -0.125 to 0.125
- down_weight: bfloat16 [5632, 2048], P('hid'), may hold values from -0.078125 to 0.078125
Outputs:
- output: bfloat16 [2048, 4, 2048], P(('seq', 'hid'))
- grad_tokens: float32 [2048, 4, 2048], P(('seq', 'hid'))
- grad_mixer_gain: float32 [2048], replicated
- grad_query_weight: float32 [2048, 2048], P(None, 'hid')
- grad_forget_weight: float32 [2048, 2048], P(None, 'hid')
- grad_input_weight: float32 [2048, 2048], P(None, 'hid')
- grad_gate_weight: float32 [2048, 2048], P(None, 'hid')
- grad_lower_bound: float32 [2048], P('hid')
- grad_head_gain: float32 [2048], P('hid')
- grad_out_weight: float32 [2048, 2048], replicated
- grad_feed_gain: float32 [2048], replicated
- grad_feed_gate_weight: float32 [2048, 5632], P(None, 'hid')
- grad_up_weight: float32 [2048, 5632], P(None, 'hid')
- grad_down_weight: float32 [5632, 2048], P('hid')
- mean_forget: float32 [], replicated
The draws below stay inside these ranges and needn't reach their ends.
Inputs may be any that keep to these rules, and one draw needn't show every extreme that they name: `lengths`: positions at or beyond a sequence's length are padding. One sequence has length exactly 2048 and another exactly 512.
All inputs are finite; a program needn't handle non-finite values.
Results may differ from the reference program's by a relative error of at most 0.009.
The reference program's roundings to bfloat16 on the way count: a program that leaves them out, or rounds other values in their place, can miss the bound.
Values may be sent and summed in bfloat16 or wider, within the bound.
No kernel may reach another device: no remote copies, remote signals or barrier semaphores. Data moves between devices by JAX's collectives and lax.ppermute only.
A program may use at most 320 MiB of HBM per device.

```python
import math
import jax
import jax.numpy as jnp
from jax import lax

D = 2048
HEADS = 16
HDIM = 128
FF = 5632
SEQS = 4
LEN = 2048
MIN_LEN = 512


def draw_lengths(key, part):
    key = jax.random.fold_in(key, 11)
    first_key, second_key = jax.random.split(key)
    drawn_len = jax.random.randint(first_key, (SEQS,), MIN_LEN, LEN + 1)
    ranking = jax.random.permutation(second_key, SEQS)
    drawn_len = jnp.where(ranking == 0, LEN, drawn_len)
    drawn_len = jnp.where(ranking == 1, MIN_LEN, drawn_len)
    return drawn_len.astype(jnp.int32)


def draw_lower_bound(key, part):
    key = jax.random.fold_in(key, 23)
    upper_log = math.log(0.5)
    exponent = jax.random.uniform(key, (D,), jnp.float32, math.log(0.0005), upper_log)
    return (1.0 - jnp.exp(exponent)).astype(jnp.float32)


def level_of(key, shape, pieces, smallest, top_value):
    def one(dim, blocks):
        steps = jax.random.uniform(jax.random.fold_in(jax.random.fold_in(key, 6), dim), (blocks,), jnp.float32, smallest / len(pieces), top_value / len(pieces))
        return jnp.repeat(jnp.exp(steps), shape[dim] // blocks).reshape((-1,) + (1,) * (len(shape) - dim - 1))

    factor_of = one(*pieces[0])
    for cut in pieces[1:]:
        factor_of = factor_of * one(*cut)
    return factor_of


def gaussian(stream_key, extent, spread, most, pieces=(), kind=jnp.bfloat16):
    drawn = spread * jax.random.normal(stream_key, extent, jnp.float32)
    if pieces:
        drawn = drawn * level_of(stream_key, extent, pieces, -0.22, 0.18)
    return jnp.clip(drawn, -most, most).astype(kind)


def setup_inputs(seed: int = 0) -> dict:
    arg_keys = jax.random.split(jax.random.key(seed), 16)
    return {
        "tokens": gaussian(arg_keys[0], (LEN, SEQS, D), 1.0, 6.0, ((0, 32),)),
        "lengths": draw_lengths(jax.random.fold_in(arg_keys[15], 71), 0),
        "cotangent": gaussian(arg_keys[2], (LEN, SEQS, D), 1.0, 6.0, ((0, 32),)),
        "mixer_gain": jnp.clip(1.0 + 0.15 * jax.random.normal(arg_keys[3], (D,), jnp.float32), 0.25, 1.75),
        "query_weight": gaussian(arg_keys[4], (D, D), D ** -0.5, 0.125, ((1, 8),)),
        "forget_weight": gaussian(arg_keys[5], (D, D), D ** -0.5, 0.125, ((1, 8),)),
        "input_weight": gaussian(arg_keys[6], (D, D), D ** -0.5, 0.125, ((1, 8),)),
        "gate_weight": gaussian(arg_keys[7], (D, D), D ** -0.5, 0.125, ((1, 8),)),
        "lower_bound": draw_lower_bound(jax.random.fold_in(arg_keys[15], 71), 0),
        "head_gain": jnp.clip(1.0 + 0.15 * jax.random.normal(arg_keys[9], (D,), jnp.float32), 0.25, 1.75),
        "out_weight": gaussian(arg_keys[10], (D, D), D ** -0.5, 0.125),
        "feed_gain": jnp.clip(1.0 + 0.15 * jax.random.normal(arg_keys[11], (D,), jnp.float32), 0.25, 1.75),
        "feed_gate_weight": gaussian(arg_keys[12], (D, FF), D ** -0.5, 0.125, ((1, 8),)),
        "up_weight": gaussian(arg_keys[13], (D, FF), D ** -0.5, 0.125, ((1, 8),)),
        "down_weight": gaussian(arg_keys[14], (FF, D), FF ** -0.5, 0.078125, ((0, 8),)),
    }


precise = lax.Precision.HIGHEST

@jax.custom_vjp
def low(v):
    return lax.optimization_barrier(v.astype(jnp.bfloat16)).astype(jnp.float32)

@jax.custom_vjp
def low_back(v):
    return v

def low_keep(v):
    return (low(v), None)

def low_pass(kept, grad):
    return (grad,)

def back_keep(v):
    return (v, None)

def back_low(kept, grad):
    return (low(grad),)
low.defvjp(low_keep, low_pass)
low_back.defvjp(back_keep, back_low)

def rms_scale(values, scale_gain, epsilon):
    return values * lax.rsqrt(lax.optimization_barrier(jnp.mean(values * values, axis=-1, keepdims=True)) + epsilon) * scale_gain

def product(left, right):
    return jnp.einsum('lsd,de->lse', left, right, precision=precise)

def to_heads(values):
    return values.reshape(LEN, SEQS, HEADS, HDIM)

def recurrence(queries, key_rates, values):
    block_shape = (LEN // 32, 32, SEQS, HEADS, HDIM)

    def block_scan(carried, members):

        def one_step(inner_state, step_members):
            query_now, rate_now, value_now = step_members
            inner_state = (1.0 - rate_now)[..., None] * inner_state + rate_now[..., None] * value_now[..., None, :]
            return (inner_state, jnp.einsum('shk,shkv->shv', query_now, inner_state, precision=precise))
        return lax.scan(one_step, carried, members)
    initial = jnp.zeros((SEQS, HEADS, HDIM, HDIM), jnp.float32)
    _, outputs = lax.scan(jax.checkpoint(block_scan), initial, (queries.reshape(block_shape), key_rates.reshape(block_shape), values.reshape(block_shape)))
    return outputs.reshape(LEN, SEQS, HEADS, HDIM)

def reference(tokens, lengths, cotangent, mixer_gain, query_weight, forget_weight, input_weight, gate_weight, lower_bound, head_gain, out_weight, feed_gain, feed_gate_weight, up_weight, down_weight):
    valid_mask = (jnp.arange(LEN)[:, None] < lengths[None, :]).astype(jnp.float32)[..., None]

    def forward(inputs, mix_gain, query_w, forget_w, input_w, gate_w, bound, gain_heads, out_w, ffn_gain, ffn_gate_w, ffn_up_w, ffn_down_w):
        normed_in = low(rms_scale(inputs, mix_gain, 1e-06))
        queries = low_back(product(normed_in, query_w))
        forget_pre = low_back(product(normed_in, forget_w))
        values = low_back(product(normed_in, input_w))
        out_gate = low_back(product(normed_in, gate_w))
        key_rates = valid_mask * (1.0 - bound) * jax.nn.sigmoid(-forget_pre)
        mixture = recurrence(to_heads(queries), to_heads(key_rates), to_heads(values))
        scaled = mixture * lax.rsqrt(lax.optimization_barrier(jnp.mean(mixture * mixture, axis=-1, keepdims=True)) + 1e-05)
        gated_out = low(scaled.reshape(LEN, SEQS, D) * gain_heads * jax.nn.silu(out_gate) * valid_mask)
        attended = low_back(product(gated_out, out_w))
        residual = inputs + attended
        normed_feed = low(rms_scale(residual, ffn_gain, 1e-06))
        feed_gate = low_back(product(normed_feed, ffn_gate_w))
        feed_up = low_back(product(normed_feed, ffn_up_w))
        hidden = low(jax.nn.silu(feed_gate) * feed_up)
        result = residual + low_back(product(hidden, ffn_down_w))
        forget_total = jnp.sum(valid_mask * (1.0 - key_rates))
        return (result, forget_total)
    primals = [tokens.astype(jnp.float32), mixer_gain.astype(jnp.float32), query_weight.astype(jnp.float32), forget_weight.astype(jnp.float32), input_weight.astype(jnp.float32), gate_weight.astype(jnp.float32), lower_bound.astype(jnp.float32), head_gain.astype(jnp.float32), out_weight.astype(jnp.float32), feed_gain.astype(jnp.float32), feed_gate_weight.astype(jnp.float32), up_weight.astype(jnp.float32), down_weight.astype(jnp.float32)]
    result, pullback, forget_total = jax.vjp(forward, *primals, has_aux=True)
    gradients = pullback(cotangent.astype(jnp.float32))
    mean_forget = forget_total / (D * jnp.sum(lengths).astype(jnp.float32))
    return (result.astype(jnp.bfloat16), gradients[0], gradients[1], gradients[2], gradients[3], gradients[4], gradients[5], gradients[6], gradients[7], gradients[8], gradients[9], gradients[10], gradients[11], gradients[12], mean_forget)
```

```python
import functools

import jax
import jax.numpy as jnp
import numpy as np
from jax import lax
from jax.experimental import pallas as pl
from jax.experimental.pallas import tpu as pltpu
from jax.sharding import PartitionSpec as P

HDIM = 128
F32 = jnp.float32
BF = jnp.bfloat16
VMEM = 60 * 1024 * 1024

NN = (((1,), (0,)), ((), ()))
NT = (((1,), (1,)), ((), ()))
TN = (((0,), (0,)), ((), ()))


def dot(a, b, dims):
    return lax.dot_general(a, b, dims, preferred_element_type=F32)


def halves(a):
    high = a.astype(BF)
    return high, (a - high.astype(F32)).astype(BF)


def dot3(a, b, dims):
    ah, al = halves(a)
    bh, bl = halves(b)
    return dot(ah, bh, dims) + (dot(ah, bl, dims) + dot(al, bh, dims))


def summed(mask, a):
    high, rest = halves(a)
    ones = mask.astype(BF)
    return dot(ones, high, NN) + dot(ones, rest, NN)


def tie(x, *after):
    return lax.optimization_barrier((x, after))[0]


def hop(array, mask):
    count = lax.axis_size("hid")
    return lax.ppermute(array, "hid", [(i, i ^ mask) for i in range(count)])


def masks(count):
    links = [1 << b for b in range(1, count.bit_length() - 1)]
    return [1] + links, [1] + links[1:] + links[:1]


def b_offsets(count):
    _, mask_b = masks(count)
    table = np.zeros(count, np.int32)
    for t in range(count):
        for bit, mask in enumerate(mask_b):
            if t >> bit & 1:
                table[t] ^= mask
    return table


class Gather:
    def __init__(self, a, b):
        self.mask_a, self.mask_b = masks(lax.axis_size("hid"))
        self.a, self.b = a[None], b[None]

    def links(self, last, after=()):
        bits = range(1, len(self.mask_a))[-1:] if last else range(1, len(self.mask_a) - 1)
        for bit in bits:
            a, b = (tie((self.a, self.b), *after) if after else (self.a, self.b))
            got_a, got_b = hop(a, self.mask_a[bit]), hop(b, self.mask_b[bit])
            if last:
                self.late = (got_a, got_b)
            else:
                self.a = jnp.concatenate([self.a, got_a])
                self.b = jnp.concatenate([self.b, got_b])

    def early(self):
        return [self.a, self.b, hop(self.a, 1), hop(self.b, 1)]

    def other(self, after=()):
        sent = tie(self.late, *after) if after else self.late
        return [hop(x, 1) for x in sent]


class Scatter:
    def __init__(self, odd):
        self.count = lax.axis_size("hid")
        self.masks = masks(self.count)
        self.got = hop(odd, 1)

    def first(self, even):
        self.kept = [[even[ab], self.got[ab]] for ab in range(2)]
        self.bit = len(self.masks[0]) - 1
        return self.step()

    def step(self):
        half = self.kept[0][0].shape[0] // 2
        sends = [
            sum(x[half:].astype(F32) for x in kept).astype(BF) for kept in self.kept
        ]
        got = [hop(send, mask[self.bit]) for send, mask in zip(sends, self.masks)]
        self.kept = [[x[:half] for x in kept] + [g] for kept, g in zip(self.kept, got)]
        self.bit -= 1
        return sends

    def more(self):
        return self.bit >= 1

    def result(self):
        return jnp.concatenate(
            [sum(x[0].astype(F32) for x in kept) for kept in self.kept], axis=0
        )


class Sums:
    def __init__(self):
        count = lax.axis_size("seq")
        half = count // 2
        self.place = lax.axis_index("seq")
        inward = [[(i, i + 1), (count - 1 - i, count - 2 - i)] for i in range(half - 1)]
        middle = [[(half - 1, half), (half, half - 1)]]
        self.pairs = inward + middle + [[(b, a) for a, b in pair] for pair in inward[::-1]]
        self.adding = half
        self.last = [None] * len(self.pairs)
        self.flying = []
        self.count = count

    def start(self, piece, stage):
        value = piece["total"]
        if self.last[stage] is not None:
            value = tie(value, self.last[stage])
        piece["got"] = self.last[stage] = lax.ppermute(value, "seq", self.pairs[stage])
        piece["stage"] = stage

    def push(self, value):
        piece = {"total": value}
        self.start(piece, 0)
        self.flying.append(piece)
        return piece

    def tick(self, line):
        for piece in list(self.flying)[::-1]:
            self.turn(piece, line)

    def turn(self, piece, line):
        stage = piece["stage"]
        total, got = piece["total"], piece["got"]
        if stage < self.adding:
            total = line(lambda a, b: (a.astype(F32) + b.astype(F32)).astype(BF), total, got)
        else:
            (target, other) = [b for _, b in self.pairs[stage]]
            mine = (self.place == target) | (self.place == other)
            if stage + 1 < len(self.pairs):
                total = line(lambda a, b: jnp.where(mine, b, a), total, got)
            else:
                total = jnp.where(mine, got, total)
        piece["total"] = total
        if stage + 1 < len(self.pairs):
            self.start(piece, stage + 1)
        else:
            self.flying.remove(piece)

    def drain(self, line):
        while self.flying:
            self.tick(line)


class Line:
    def __init__(self):
        self.token = None

    def __call__(self, function, *args):
        if self.token is not None:
            args = tie(args, self.token)
        result = function(*args)
        self.token = jax.tree.leaves(result)[0]
        return result


def everywhere(value, axis):
    count = lax.axis_size(axis)
    mask = 1
    while mask < count:
        value = value + lax.ppermute(value, axis, [(i, i ^ mask) for i in range(count)])
        mask *= 2
    return value


class Entering:
    def __init__(self, state, fade, reverse):
        self.count = lax.axis_size("seq")
        self.reverse = reverse
        self.reach, self.cover, self.fade = 1, state, fade
        self.border = None
        self.send()

    def send(self):
        step = -self.reach if self.reverse else self.reach
        pairs = [(i, i + step) for i in range(self.count) if 0 <= i + step < self.count]
        self.got = [
            lax.ppermute(self.cover.astype(BF), "seq", pairs),
            lax.ppermute(self.fade, "seq", pairs),
        ]

    def take(self, line):
        def merge(got, got_fade, cover, fade, border, border_fade):
            got = got.astype(F32)
            if border is None:
                border, border_fade = got, got_fade
            else:
                border, border_fade = border + border_fade * got, border_fade * got_fade
            return border, border_fade, cover + fade * got, fade * got_fade

        border = self.border or (None, None)
        *self.border, self.cover, self.fade = line(
            merge, *self.got, self.cover, self.fade, *border
        )
        self.reach *= 2
        if self.reach >= self.count:
            return True
        self.send()
        return False

    def finish(self, line):
        while not self.take(line):
            pass
        return self.border[0]


def stream(groups, place, count, weights, outs, body, before=None):
    chips, rows, width = groups[0][0].shape
    n_sets, n_w, n_out = len(groups), len(weights), len(outs)
    parts = len(groups[0])
    n_arrays = parts * n_sets
    steps = chips if place is None else 1
    lines = 4 * rows if place is None else chips * 2 * rows

    def kernel(*refs):
        arrays = refs[:n_arrays]
        w_refs = refs[n_arrays : n_arrays + n_w]
        refs = refs[n_arrays + n_w + (n_out if before is not None else 0) :]
        out_refs, bufs, sem = refs[:n_out], refs[n_out:-1], refs[-1]
        i = pl.program_id(0)

        def copies(k):
            chosen = [(k, part, part) for part in range(4)]
            if place is not None:
                chosen = [(c, ab, 2 * c + ab) for c in range(chips) for ab in range(2)]
            return [
                pltpu.make_async_copy(
                    arrays[parts * s + part].at[c],
                    bufs[s].at[k % 2, pl.ds(at * rows, rows)],
                    sem.at[s, k % 2, at],
                )
                for s in range(n_sets)
                for c, part, at in chosen
            ]

        for k in range(steps):

            @pl.when(i == k)
            def _(k=k):
                if k == 0:
                    for copy in copies(0):
                        copy.start()
                if k + 1 < steps:
                    for copy in copies(k + 1):
                        copy.start()
                for copy in copies(k):
                    copy.wait()

        slot = lax.rem(i, 2) if steps > 1 else 0
        results = body([buf[slot] for buf in bufs], w_refs)
        for ref, value in zip(out_refs, results):
            ref[...] = value.reshape(ref.shape).astype(ref.dtype)

    anywhere = pl.BlockSpec(memory_space=pl.ANY)
    whole = lambda w: pl.BlockSpec(w.shape, lambda i: (0, 0), pipeline_mode=pl.Buffered(1))
    given = [] if before is None else list(before)
    if place is None:
        out_spec = lambda c: pl.BlockSpec((1, 2, 2, rows, c), lambda i: (i, 0, 0, 0, 0))
    else:
        out_spec = lambda c: pl.BlockSpec((chips, 1, 2, rows, c), lambda i: (1, place, 0, 0, 0))
    return pl.pallas_call(
        kernel,
        grid=(steps,),
        in_specs=[anywhere] * n_arrays + [whole(w) for w in weights] + [anywhere] * len(given),
        out_specs=[out_spec(c) for c, _ in outs],
        out_shape=[jax.ShapeDtypeStruct((count // 2, 2, 2, rows, c), d) for c, d in outs],
        scratch_shapes=[pltpu.VMEM((min(steps, 2), lines, width), BF) for _ in groups]
        + [pltpu.SemaphoreType.DMA((n_sets, 2, lines // rows))],
        input_output_aliases={n_arrays + n_w + o: o for o in range(len(given))},
        compiler_params=pltpu.CompilerParams(vmem_limit_bytes=VMEM),
    )(*[x for s in groups for x in s], *weights, *given)


def by_slot(arrays):
    return [x.reshape((-1,) + x.shape[2:]) for x in arrays]


def head_rows(rows, out_weight, count):
    own, width = rows.shape
    cols = out_weight.shape[0] // count

    def kernel(rows_ref, weight_ref, out_ref):
        out_ref[0] = dot(rows_ref[...], weight_ref[...], NT).astype(BF)

    return pl.pallas_call(
        kernel,
        grid=(count,),
        in_specs=[
            pl.BlockSpec((own, width), lambda i: (0, 0)),
            pl.BlockSpec((cols, width), lambda i: (i, 0)),
        ],
        out_specs=pl.BlockSpec((1, own, cols), lambda i: (i, 0, 0)),
        out_shape=jax.ShapeDtypeStruct((count, own, cols), BF),
        compiler_params=pltpu.CompilerParams(vmem_limit_bytes=VMEM),
    )(rows, out_weight)


def partial_rows(lefts, weights, dims, parity):
    count, _, rows, _ = lefts[0].shape
    width = weights[0].shape[1 if dims == NN else 0]
    n = len(lefts)

    def kernel(*refs):
        total = None
        for left, weight in zip(refs[:n], refs[n : 2 * n]):
            value = left[...].reshape(2 * rows, left.shape[-1])
            part = dot(value, weight[...], dims)
            total = part if total is None else total + part
        refs[2 * n][...] = total.astype(BF).reshape(2, 1, rows, width)

    whole = lambda w: pl.BlockSpec(w.shape, lambda i: (0, 0), pipeline_mode=pl.Buffered(1))
    return pl.pallas_call(
        kernel,
        grid=(count // 2,),
        in_specs=[
            pl.BlockSpec((1, 2, rows, x.shape[-1]), lambda i: (2 * i + parity, 0, 0, 0))
            for x in lefts
        ]
        + [whole(w) for w in weights],
        out_specs=pl.BlockSpec((2, 1, rows, width), lambda i: (0, i, 0, 0)),
        out_shape=jax.ShapeDtypeStruct((2, count // 2, rows, width), BF),
        compiler_params=pltpu.CompilerParams(vmem_limit_bytes=VMEM),
    )(*lefts, *weights)


def owned_rows(left, weight, table):
    count, _, rows, depth = left.shape
    width = weight.shape[1]

    def kernel(_, left_ref, weight_ref, a_ref, b_ref):
        total = dot(left_ref[...].reshape(2 * rows, depth), weight_ref[...], NN).astype(BF)
        a_ref[...] = total[:rows]
        b_ref[...] = total[rows:]

    return pl.pallas_call(
        kernel,
        grid_spec=pltpu.PrefetchScalarGridSpec(
            num_scalar_prefetch=1,
            grid=(count,),
            in_specs=[
                pl.BlockSpec((1, 2, rows, depth), lambda t, tab: (t, 0, 0, 0)),
                pl.BlockSpec(weight.shape, lambda t, tab: (0, 0), pipeline_mode=pl.Buffered(1)),
            ],
            out_specs=[
                pl.BlockSpec((rows, width), lambda t, tab: (tab[t], 0)),
                pl.BlockSpec((rows, width), lambda t, tab: (tab[count + t], 0)),
            ],
        ),
        out_shape=[jax.ShapeDtypeStruct((count * rows, width), BF)] * 2,
        compiler_params=pltpu.CompilerParams(vmem_limit_bytes=VMEM),
    )(table, left, weight)


def attend(moved, out_weight, own_rows, gain):
    count, rows, cols = moved.shape
    depth, width = out_weight.shape
    block = 512
    steps = width // block

    def kernel(moved_ref, weight_ref, own_ref, gain_ref, res_ref, normed_ref, left_ref):
        i = pl.program_id(0)

        @pl.when(i == 0)
        def _():
            for s in range(count):
                left_ref[:, s * cols : (s + 1) * cols] = moved_ref[s]

        part = dot(left_ref[...], weight_ref[...], NN)
        for k in range(steps):

            @pl.when(i == k)
            def _(k=k):
                at = slice(k * block, (k + 1) * block)
                res_ref[:, at] = own_ref[:, at].astype(F32) + part

        @pl.when(i == steps - 1)
        def _():
            value = res_ref[...]
            scale = lax.rsqrt(jnp.mean(value * value, axis=-1, keepdims=True) + 1e-06)
            normed_ref[...] = (value * scale * gain_ref[...]).astype(BF)

    return pl.pallas_call(
        kernel,
        grid=(steps,),
        in_specs=[
            pl.BlockSpec((count, rows, cols), lambda i: (0, 0, 0)),
            pl.BlockSpec((depth, block), lambda i: (0, i)),
            pl.BlockSpec((rows, width), lambda i: (0, 0)),
            pl.BlockSpec((1, width), lambda i: (0, 0)),
        ],
        out_specs=[pl.BlockSpec((rows, width), lambda i: (0, 0))] * 2,
        out_shape=[
            jax.ShapeDtypeStruct((rows, width), F32),
            jax.ShapeDtypeStruct((rows, width), BF),
        ],
        scratch_shapes=[pltpu.VMEM((rows, depth), BF)],
        compiler_params=pltpu.CompilerParams(vmem_limit_bytes=VMEM),
    )(moved, out_weight, own_rows, gain)


class Scan:
    def __init__(self, count, seqs, rows, cols, table, base, lengths, lower):
        self.count, self.rows, self.cols = count, rows, cols
        self.per = seqs // 2
        self.heads = cols // HDIM
        self.total = seqs * self.heads
        self.scalars = jnp.concatenate([table, base[None], lengths]).astype(jnp.int32)
        self.lower = lower.reshape(1, cols)

    def slots(self, part, width, reverse):
        n = self.count

        def of(ab):
            def place(p, sc):
                p = n - 1 - p if reverse else p
                return (sc[ab * n + p], ab, 0, part)

            return pl.BlockSpec((1, 1, self.per * self.rows, width), place)

        return [of(0), of(1)]

    def chunk(self, shape, reverse):
        n = self.count
        zeros = (0,) * (len(shape) - 1)
        return pl.BlockSpec(
            (1,) + tuple(shape[1:]), lambda p, sc: ((n - 1 - p if reverse else p),) + zeros
        )

    def whole(self, shape):
        zeros = (0,) * len(shape)
        return pl.BlockSpec(tuple(shape), lambda p, sc: zeros)

    def call(self, kernel, in_specs, out_specs, out_shape, scratch, args):
        return pl.pallas_call(
            kernel,
            grid_spec=pltpu.PrefetchScalarGridSpec(
                num_scalar_prefetch=1,
                grid=(self.count,),
                in_specs=in_specs,
                out_specs=out_specs,
                scratch_shapes=scratch,
            ),
            out_shape=out_shape,
            compiler_params=pltpu.CompilerParams(vmem_limit_bytes=VMEM),
        )(self.scalars, *args)

    def units(self):
        for ab in range(2):
            for s in range(self.per):
                yield ab, s, slice(s * self.rows, (s + 1) * self.rows)

    def state(self, ab, s, h):
        return (ab * self.per + s) * self.heads + h

    def valid(self, sc, p, ab, s):
        n = self.count
        pos = sc[2 * n] + p * self.rows + lax.broadcasted_iota(jnp.int32, (self.rows, 1), 0)
        return (pos < sc[2 * n + 1 + ab * self.per + s]).astype(F32)

    def triangle(self):
        r = lax.broadcasted_iota(jnp.int32, (self.rows, self.rows), 0)
        c = lax.broadcasted_iota(jnp.int32, (self.rows, self.rows), 1)
        return r >= c, r <= c

    def rates(self, forget, lower, valid):
        negative = jax.nn.sigmoid(-forget)
        keys = valid * (1.0 - lower) * negative
        down, _ = self.triangle()
        cum = summed(down.astype(F32), jnp.log(1.0 - keys))
        return negative, keys, cum

    def ends(self, joint):
        n, total, c = self.count, self.total, self.cols

        def kernel(sc, fa_ref, fb_ref, va_ref, vb_ref, lower_ref, end_ref, fade_ref, sum_ref):
            p = pl.program_id(0)

            @pl.when(p == 0)
            def _():
                end_ref[...] = jnp.zeros(end_ref.shape, F32)
                fade_ref[...] = jnp.ones(fade_ref.shape, F32)
                sum_ref[...] = jnp.zeros(sum_ref.shape, F32)

            gates = jnp.zeros((1, c), F32)
            for ab, s, sp in self.units():
                f_ref, v_ref = (fa_ref, fb_ref)[ab], (va_ref, vb_ref)[ab]
                valid = self.valid(sc, p, ab, s)
                _, keys, cum = self.rates(f_ref[0, 0, sp], lower_ref[...], valid)
                last = cum[self.rows - 1 :]
                gates += jnp.sum(valid * (1.0 - keys), axis=0, keepdims=True)
                to_end = keys * jnp.exp(last - cum)
                fade = jnp.exp(last)
                values = v_ref[0, 0, sp]
                for h in range(self.heads):
                    at = self.state(ab, s, h)
                    ch = slice(h * HDIM, (h + 1) * HDIM)
                    grown = dot3(values[:, ch], to_end[:, ch], TN)
                    end_ref[at] = end_ref[at] * fade[:, ch] + grown
                    fade_ref[at] = fade_ref[at] * fade[:, ch]
            sum_ref[...] += gates

        shapes = [
            jax.ShapeDtypeStruct((total, HDIM, HDIM), F32),
            jax.ShapeDtypeStruct((total, 1, HDIM), F32),
            jax.ShapeDtypeStruct((1, c), F32),
        ]
        return self.call(
            kernel,
            self.slots(1, c, False) + self.slots(2, c, False) + [self.whole((1, c))],
            [self.whole(x.shape) for x in shapes],
            shapes,
            [],
            (joint,) * 4 + (self.lower,),
        )

    def forward(self, joint):
        n, total, c = self.count, self.total, self.cols
        rows = self.per * self.rows

        def kernel(sc, ja_ref, jb_ref, lower_ref, mix_ref, reach_ref, start_ref, fade_ref, state_ref, kept_ref):
            p = pl.program_id(0)

            @pl.when(p == 0)
            def _():
                state_ref[...] = jnp.zeros(state_ref.shape, F32)
                kept_ref[...] = jnp.ones(kept_ref.shape, F32)

            down, _ = self.triangle()
            mid_row = self.rows // 2 - 1
            for ab, s, sp in self.units():
                joint_ref = (ja_ref, jb_ref)[ab]
                valid = self.valid(sc, p, ab, s)
                queries = joint_ref[0, 0, sp, 0:c]
                values = joint_ref[0, 0, sp, 2 * c : 3 * c]
                _, keys, cum = self.rates(joint_ref[0, 0, sp, c : 2 * c], lower_ref[...], valid)
                mid, last = cum[mid_row : mid_row + 1], cum[self.rows - 1 :]
                q_mid = queries * jnp.exp(cum - mid)
                k_mid = keys * jnp.exp(mid - cum)
                q_start = q_mid * jnp.exp(mid)
                to_end = k_mid * jnp.exp(last - mid)
                fade = jnp.exp(last)
                for h in range(self.heads):
                    at = self.state(ab, s, h)
                    ch = slice(h * HDIM, (h + 1) * HDIM)
                    state, kept = state_ref[at], kept_ref[at]
                    start_ref[0, at] = state
                    fade_ref[0, at] = kept
                    scores = jnp.where(down, dot3(q_mid[:, ch], k_mid[:, ch], NT), 0.0)
                    mix = dot3(scores, values[:, ch], NN) + dot3(q_start[:, ch], state, NT)
                    state_ref[at] = state * fade[:, ch] + dot3(values[:, ch], to_end[:, ch], TN)
                    mix_ref[0, ab, sp, ch] = mix
                    reach_ref[0, ab, sp, ch] = q_start[:, ch] * kept
                    kept_ref[at] = kept * fade[:, ch]

        shapes = [
            jax.ShapeDtypeStruct((n, 2, rows, c), F32),
            jax.ShapeDtypeStruct((n, 2, rows, c), F32),
            jax.ShapeDtypeStruct((n, total, HDIM, HDIM), F32),
            jax.ShapeDtypeStruct((n, total, 1, HDIM), F32),
        ]
        return self.call(
            kernel,
            self.slots(0, 4 * c, False) + [self.whole((1, c))],
            [self.chunk(x.shape, False) for x in shapes],
            shapes,
            [pltpu.VMEM((total, HDIM, HDIM), F32), pltpu.VMEM((total, 1, HDIM), F32)],
            (joint, joint, self.lower),
        )

    def finish(self, joint, mixture, reach, initial, head_gain):
        n, total, c = self.count, self.total, self.cols
        rows = self.per * self.rows

        def kernel(sc, ga_ref, gb_ref, local_ref, reach_ref, init_ref, gain_ref, mix_ref, out_ref):
            p = pl.program_id(0)
            for ab, s, sp in self.units():
                gates = (ga_ref, gb_ref)[ab][0, 0, sp]
                valid = self.valid(sc, p, ab, s)
                scale = gain_ref[...] * (gates * jax.nn.sigmoid(gates)) * valid
                for h in range(self.heads):
                    at = self.state(ab, s, h)
                    ch = slice(h * HDIM, (h + 1) * HDIM)
                    mix = local_ref[0, ab, sp, ch] + dot3(reach_ref[0, ab, sp, ch], init_ref[at], NT)
                    rho = lax.rsqrt(jnp.mean(mix * mix, axis=-1, keepdims=True) + 1e-05)
                    mix_ref[0, ab, sp, ch] = mix
                    out_ref[0, ab, sp, ch] = (mix * rho * scale[:, ch]).astype(BF)

        shapes = [
            jax.ShapeDtypeStruct((n, 2, rows, c), F32),
            jax.ShapeDtypeStruct((n, 2, rows, c), BF),
        ]
        chunk = self.chunk(mixture.shape, False)
        return self.call(
            kernel,
            self.slots(3, c, False)
            + [chunk, chunk, self.whole((total, HDIM, HDIM)), self.whole((1, c))],
            [chunk, chunk],
            shapes,
            [],
            (joint, joint, mixture, reach, initial, head_gain.reshape(1, c)),
        )

    def finish_back(self, joint, mixture, grad_gated, head_gain):
        n, total, c = self.count, self.total, self.cols
        rows = self.per * self.rows

        def kernel(
            sc, qa_ref, qb_ref, fa_ref, fb_ref, ga_ref, gb_ref, mix_ref, grad_ref,
            lower_ref, gain_ref, gm_ref, gate_ref, head_ref, reach_ref,
        ):
            step = pl.program_id(0)
            p = n - 1 - step

            @pl.when(step == 0)
            def _():
                head_ref[...] = jnp.zeros(head_ref.shape, F32)
                reach_ref[...] = jnp.zeros(reach_ref.shape, F32)

            gain = gain_ref[...]
            heads = [jnp.zeros((1, HDIM), F32)] * self.heads
            for ab, s, sp in self.units():
                q_ref, f_ref, g_ref = (qa_ref, qb_ref)[ab], (fa_ref, fb_ref)[ab], (ga_ref, gb_ref)[ab]
                slot = sc[ab * n + p]
                valid = self.valid(sc, p, ab, s)
                _, _, cum = self.rates(f_ref[0, 0, sp], lower_ref[...], valid)
                q_start = q_ref[0, 0, sp] * jnp.exp(cum)
                fade = jnp.exp(cum[self.rows - 1 :])
                gates = g_ref[0, 0, sp]
                sig = jax.nn.sigmoid(gates)
                arriving = grad_ref[0, ab, sp].astype(F32) * valid
                e = arriving * (gates * sig)
                slope = arriving * gain * sig * (1.0 + gates * (1.0 - sig))
                for h in range(self.heads):
                    at = self.state(ab, s, h)
                    ch = slice(h * HDIM, (h + 1) * HDIM)
                    mix = mix_ref[0, ab, sp, ch]
                    rho = lax.rsqrt(jnp.mean(mix * mix, axis=-1, keepdims=True) + 1e-05)
                    scaled = mix * rho
                    heads[h] += jnp.sum(e[:, ch] * scaled, axis=0, keepdims=True)
                    ge = gain[:, ch] * e[:, ch]
                    gm = rho * ge - mix * (rho * rho * rho) * jnp.mean(
                        mix * ge, axis=-1, keepdims=True
                    )
                    gm_ref[0, ab, sp, ch] = gm
                    gate_ref[slot, ab, sp, ch] = (scaled * slope[:, ch]).astype(BF)
                    reach_ref[at] = reach_ref[at] * fade[:, ch] + dot3(gm, q_start[:, ch], TN)
            for h in range(self.heads):
                head_ref[:, h * HDIM : (h + 1) * HDIM] += heads[h]

        shapes = [
            jax.ShapeDtypeStruct((n, 2, rows, c), F32),
            jax.ShapeDtypeStruct((n, 2, rows, c), BF),
            jax.ShapeDtypeStruct((1, c), F32),
            jax.ShapeDtypeStruct((total, HDIM, HDIM), F32),
        ]
        slots = lambda part: self.slots(part, c, True)
        return self.call(
            kernel,
            slots(0) + slots(1) + slots(3)
            + [self.chunk(mixture.shape, True), self.chunk(mixture.shape, True)]
            + [self.whole((1, c)), self.whole((1, c))],
            [self.chunk(shapes[0].shape, True)] + [self.whole(x.shape) for x in shapes[1:]],
            shapes,
            [],
            (joint,) * 6 + (mixture, grad_gated, self.lower, head_gain.reshape(1, c)),
        )

    def backward(self, joint, grad_mix, starts, fades, initial, final, leaving):
        n, total, c = self.count, self.total, self.cols
        rows = self.per * self.rows

        def kernel(
            sc, qa_ref, qb_ref, fa_ref, fb_ref, va_ref, vb_ref, gm_ref, start_ref, fade_ref,
            init_ref, final_ref, leave_ref, lower_ref, out_ref, low_ref, back_ref, end_ref,
        ):
            step = pl.program_id(0)
            p = n - 1 - step

            @pl.when(step == 0)
            def _():
                back_ref[...] = leave_ref[...]
                end_ref[...] = final_ref[...]
                low_ref[...] = jnp.zeros(low_ref.shape, F32)

            down, up = self.triangle()
            mid_row = self.rows // 2 - 1
            room = 1.0 - lower_ref[...]
            lows = [jnp.zeros((1, HDIM), F32)] * self.heads
            for ab, s, sp in self.units():
                q_ref, f_ref, v_ref = (qa_ref, qb_ref)[ab], (fa_ref, fb_ref)[ab], (va_ref, vb_ref)[ab]
                slot = sc[ab * n + p]
                valid = self.valid(sc, p, ab, s)
                queries, values = q_ref[0, 0, sp], v_ref[0, 0, sp]
                forget = f_ref[0, 0, sp]
                neg, keys, cum = self.rates(forget, lower_ref[...], valid)
                mid, last = cum[mid_row : mid_row + 1], cum[self.rows - 1 :]
                from_mid, to_mid = jnp.exp(cum - mid), jnp.exp(mid - cum)
                start_mid, mid_last = jnp.exp(mid), jnp.exp(last - mid)
                q_mid, k_mid = queries * from_mid, keys * to_mid
                q_start, k_last = q_mid * start_mid, k_mid * mid_last
                fade = jnp.exp(last)
                pos = jax.nn.sigmoid(forget)
                for h in range(self.heads):
                    at = self.state(ab, s, h)
                    ch = slice(h * HDIM, (h + 1) * HDIM)
                    gm, val = gm_ref[0, ab, sp, ch], values[:, ch]
                    start, back = start_ref[0, at] + fade_ref[0, at] * init_ref[at], back_ref[at]
                    scores = jnp.where(down, dot3(q_mid[:, ch], k_mid[:, ch], NT), 0.0)
                    pull = jnp.where(down, dot3(gm, val, NT), 0.0)
                    gq = from_mid[:, ch] * (
                        dot3(pull, k_mid[:, ch], NN) + dot3(gm, start, NN) * start_mid[:, ch]
                    )
                    gv = dot3(scores, gm, TN) + dot3(k_last[:, ch], back, NT)
                    gk = to_mid[:, ch] * (
                        dot3(pull, q_mid[:, ch], TN) + dot3(val, back, NN) * mid_last[:, ch]
                    )
                    at_end = jnp.sum(back * end_ref[at], axis=0, keepdims=True)
                    fading = at_end + summed(
                        up.astype(F32), queries[:, ch] * gq - keys[:, ch] * gk
                    )
                    gk = gk - fading / (1.0 - keys[:, ch])
                    gk_valid = gk * valid * neg[:, ch]
                    lows[h] += jnp.sum(gk_valid, axis=0, keepdims=True)
                    gf = -gk_valid * room[:, ch] * pos[:, ch]
                    for part, value in enumerate((gq, gf, gv)):
                        at_col = part * c + h * HDIM
                        out_ref[slot, ab, sp, at_col : at_col + HDIM] = value.astype(BF)
                    end_ref[at] = start
                    back_ref[at] = back * fade[:, ch] + dot3(gm, q_start[:, ch], TN)
            for h in range(self.heads):
                low_ref[:, h * HDIM : (h + 1) * HDIM] -= lows[h]

        shapes = [
            jax.ShapeDtypeStruct((n, 2, rows, 3 * c), BF),
            jax.ShapeDtypeStruct((1, c), F32),
        ]
        slots = lambda part: self.slots(part, c, True)
        states = self.whole((total, HDIM, HDIM))
        return self.call(
            kernel,
            slots(0) + slots(1) + slots(2)
            + [self.chunk(grad_mix.shape, True), self.chunk(starts.shape, True), self.chunk(fades.shape, True)]
            + [states] * 3
            + [self.whole((1, c))],
            [self.whole(x.shape) for x in shapes],
            shapes,
            [pltpu.VMEM((total, HDIM, HDIM), F32)] * 2,
            (joint,) * 6 + (grad_mix, starts, fades, initial, final, leaving, self.lower),
        )


def norm_back(values, gain, grad, epsilon):
    scale = lax.rsqrt(jnp.mean(values * values, axis=-1, keepdims=True) + epsilon)
    pulled = gain * grad
    grad_values = scale * pulled - values * (scale * scale * scale) * jnp.mean(
        values * pulled, axis=-1, keepdims=True
    )
    return grad_values, jnp.sum(values * scale * grad, axis=0)


def weight_grad(left, right):
    return lax.dot_general(left, right, TN, preferred_element_type=F32).astype(BF)


def shards(
    tokens,
    lengths,
    cotangent,
    mixer_gain,
    query_weight,
    forget_weight,
    input_weight,
    gate_weight,
    lower_bound,
    head_gain,
    out_weight,
    feed_gain,
    feed_gate_weight,
    up_weight,
    down_weight,
):
    count = lax.axis_size("hid")
    me = lax.axis_index("hid")
    rows, seqs, width = tokens.shape
    cols = query_weight.shape[1]
    units = feed_gate_weight.shape[1]
    base = lax.axis_index("seq") * (rows * count)
    own = seqs * rows
    cut = own // 2

    def halves_of(array):
        return array[:cut], array[cut:]

    def to_rows(array):
        return jnp.transpose(array, (1, 0, 2)).reshape(own, width)

    def from_rows(array):
        return jnp.transpose(array.reshape(seqs, rows, width), (1, 0, 2))

    flat = lambda x: x.reshape(-1, x.shape[-1])
    offsets = jnp.concatenate([jnp.arange(count), jnp.asarray(b_offsets(count))]) ^ me
    inverse = np.argsort(b_offsets(count)).astype(np.int32)
    places = jnp.arange(count) ^ me
    table = jnp.concatenate([places, jnp.asarray(inverse)[places]])
    scan = Scan(count, seqs, rows, cols, table, base, lengths, lower_bound)
    line = Line()
    gate_t, up_t = feed_gate_weight.T, up_weight.T

    own_rows = to_rows(tokens)
    inputs = own_rows.astype(F32)
    in_scale = lax.rsqrt(jnp.mean(inputs * inputs, axis=-1, keepdims=True) + 1e-06)
    normed_in = (inputs * in_scale * mixer_gain).astype(BF)
    going = Gather(*halves_of(normed_in))
    going.links(False)
    going.links(True)
    joint_weights = (query_weight, forget_weight, input_weight, gate_weight)
    joint_out = [(4 * cols, F32), (width, BF)]

    def project(group, place, before=None):
        def body(xs, w_refs):
            return [jnp.concatenate([dot(xs[0], w[...], NN) for w in w_refs], axis=1), xs[0]]

        return line(
            lambda group, before: stream(
                [group], place, count, joint_weights, joint_out, body, before
            ),
            group,
            before,
        )

    part = project(going.early(), None)
    cot_rows = tie(to_rows(cotangent), part[0])
    other = going.other((part[0], cot_rows))
    part = project(list(going.late), 0, part)
    cots = Gather(*tie(halves_of(cot_rows), other))
    cots.links(False)
    joint, in_rows = by_slot(project(other, 1, part))
    ends, fade, gate_sums = line(scan.ends, joint)
    entry = Entering(ends, fade, False)
    cots.links(True, (ends,))
    mixture, reach, starts, fades = line(scan.forward, joint)
    initial = entry.finish(line)
    mixture, gated_p = line(scan.finish, joint, mixture, reach, initial, head_gain)
    moved = lax.all_to_all(
        gated_p.reshape(count, own, cols), "hid", split_axis=0, concat_axis=0, tiled=True
    )
    cot_early = tie((cots.a, cots.b), gated_p)
    cot_early = list(cot_early) + [hop(x, 1) for x in cot_early]
    cot_other = cots.other((gated_p,))
    residual, normed_feed = line(
        lambda m, _: attend(m, out_weight, own_rows, feed_gain.reshape(1, width)),
        moved,
        (cot_early, cot_other),
    )

    going = Gather(*halves_of(normed_feed))
    going.links(False)
    going.links(True)
    feed_weights = (gate_t, up_t, down_weight)
    feed_shapes = [(units, BF)] * 3 + [(width, BF)] * 2

    def feed(group, cot_group, place, before=None):
        def body(xs, w_refs):
            gate = dot(xs[0], w_refs[0][...], NT)
            up = dot(xs[0], w_refs[1][...], NT)
            grad_hidden = dot(xs[1], w_refs[2][...], NT)
            sig = jax.nn.sigmoid(gate)
            silu = gate * sig
            grad_gate = grad_hidden * up * sig * (1.0 + gate * (1.0 - sig))
            return [silu * up, grad_gate, grad_hidden * silu, xs[0], xs[1]]

        return line(
            lambda group, cot_group, before: stream(
                [group, cot_group], place, count, feed_weights, feed_shapes, body, before
            ),
            group,
            cot_group,
            before,
        )

    part = feed(going.early(), cot_early, None)
    other = going.other((part[0],))
    part = feed(list(going.late), list(cots.late), 0, part)
    hidden, grad_feed_gate, grad_up, feed_rows, grad_rows = by_slot(
        feed(other, cot_other, 1, part)
    )
    hidden_f, gate_f, up_f = flat(hidden), flat(grad_feed_gate), flat(grad_up)
    feed_f, grad_f = flat(feed_rows), flat(grad_rows)
    sums = Sums()
    backs = lambda parity: line(
        lambda *a: partial_rows(a, (gate_t, up_t), NN, parity), grad_feed_gate, grad_up
    )
    shrink = Scatter(backs(1))
    even = backs(0)
    down_w = sums.push(line(weight_grad, hidden_f, grad_f))
    line(shrink.first, even)
    gate_w = line(weight_grad, gate_f, feed_f)
    while shrink.more():
        line(lambda *_: shrink.step())
    up_w = line(weight_grad, up_f, feed_f)

    def after_feed(grad):
        cot = to_rows(cotangent).astype(F32)
        grad_part, grad_gain = norm_back(residual, feed_gain, grad, 1e-06)
        grad_residual = cot + grad_part
        return grad_residual.astype(BF), grad_residual, grad_gain

    grad_attended, grad_residual, grad_feed_gain = line(after_feed, shrink.result())

    sent = line(lambda rows: head_rows(rows, out_weight, count), grad_attended)
    grad_gated = lax.all_to_all(sent, "hid", split_axis=0, concat_axis=0, tiled=True)
    sums.tick(line)
    gate_w = sums.push(gate_w)
    out_full = line(
        lambda m, g: lax.dot_general(
            m, g, (((1,), (0,)), ((), ())), preferred_element_type=F32
        ).astype(BF),
        moved,
        grad_attended,
    )
    grad_mix, grad_gate, grad_head, reach = line(
        scan.finish_back, joint, mixture, grad_gated.reshape(mixture.shape), head_gain
    )
    exit_ = Entering(reach, fade, True)
    in_f = flat(in_rows)
    mix_gate = line(weight_grad, in_f, flat(grad_gate))
    spread = lambda x: lax.psum_scatter(x, "hid", scatter_dimension=0, tiled=True)
    out_part = spread(tie(out_full.reshape(count * cols, width), mix_gate))
    leaving_done = exit_.take(line)
    feed_a, feed_b = line(owned_rows, hidden, down_weight, offsets)
    feed_out = jnp.concatenate([spread(feed_a), spread(feed_b)], axis=0)
    sums.tick(line)
    up_w = sums.push(up_w)
    leaving = exit_.border[0] if leaving_done else exit_.finish(line)
    final = ends + fade * initial
    grad_three, grad_lower = line(
        scan.backward, joint, grad_mix, starts, fades, initial, final, leaving
    )
    three_f = flat(grad_three)
    quarter = width // 4
    three = lambda i: line(
        lambda x, g: weight_grad(x[:, i * quarter : (i + 1) * quarter], g), in_f, three_f
    )
    threes = [three(0), three(1)]
    sums.tick(line)
    out_part = sums.push(out_part)
    joint_three = jnp.concatenate(joint_weights[:3], axis=1)
    backs = lambda parity: line(
        lambda *a: partial_rows(a, (joint_three, gate_weight), NT, parity), grad_three, grad_gate
    )
    shrink = Scatter(backs(1))
    threes += [three(2), three(3)]
    sums.tick(line)
    mix_gate = sums.push(mix_gate)
    even = backs(0)
    line(shrink.first, even)
    sums.tick(line)
    threes[0] = sums.push(threes[0])
    while shrink.more():
        line(lambda *_: shrink.step())
    sums.tick(line)
    threes[1] = sums.push(threes[1])
    grad_in, grad_mixer = line(lambda g: norm_back(inputs, mixer_gain, g, 1e-06), shrink.result())
    grad_tokens = line(lambda a, b: from_rows(a + b), grad_residual, grad_in)
    small = everywhere(
        jnp.concatenate([grad_mixer, grad_feed_gain, jnp.sum(gate_sums).reshape(1)]), "hid"
    )
    sums.tick(line)
    threes[2] = sums.push(threes[2])
    small = everywhere(jnp.concatenate([small, grad_lower[0], grad_head[0]]), "seq")
    heads = small[2 * width + 1 :]
    sums.tick(line)
    threes[3] = sums.push(threes[3])
    output = line(lambda a, b: from_rows((a + b).astype(BF)), residual, feed_out)
    gathered_out = lax.all_gather(out_part["total"], "hid", axis=0, tiled=True)
    sums.tick(line)
    grad_out = line(lambda x: x.astype(F32), gathered_out)
    sums.drain(line)
    total = lambda *parts: jnp.concatenate([p["total"] for p in parts], axis=0).astype(F32)
    three_w = total(*threes)
    mean_forget = small[2 * width] / (width * jnp.sum(lengths).astype(F32))
    return (
        output,
        grad_tokens,
        small[:width],
        three_w[:, :cols],
        three_w[:, cols : 2 * cols],
        three_w[:, 2 * cols :],
        total(mix_gate),
        heads[:cols],
        heads[cols:],
        grad_out,
        small[width : 2 * width],
        total(gate_w).T,
        total(up_w).T,
        total(down_w),
        mean_forget,
    )


def solution(mesh):
    rows = P(("seq", "hid"), None, None)
    columns = P(None, "hid")
    return jax.shard_map(
        shards,
        mesh=mesh,
        in_specs=(
            rows,
            P(),
            rows,
            P(),
            columns,
            columns,
            columns,
            columns,
            P("hid"),
            P("hid"),
            P(),
            P(),
            columns,
            columns,
            P("hid", None),
        ),
        out_specs=(
            rows,
            rows,
            P(),
            columns,
            columns,
            columns,
            columns,
            P("hid"),
            P("hid"),
            P(),
            P(),
            columns,
            columns,
            P("hid", None),
            P(),
        ),
        check_vma=False,
    )
```

```python
import functools

import jax
import jax.numpy as jnp
import numpy as np
from jax import lax
from jax.experimental import pallas as pl
from jax.experimental.pallas import tpu as pltpu
from jax.sharding import PartitionSpec as P

HDIM = 128
F32 = jnp.float32
BF = jnp.bfloat16
VMEM = 60 * 1024 * 1024

NN = (((1,), (0,)), ((), ()))
NT = (((1,), (1,)), ((), ()))
TN = (((0,), (0,)), ((), ()))


def dot(a, b, dims):
    return lax.dot_general(a, b, dims, preferred_element_type=F32)


def halves(a):
    high = a.astype(BF)
    return high, (a - high.astype(F32)).astype(BF)


def dot3(a, b, dims):
    ah, al = halves(a)
    bh, bl = halves(b)
    return dot(ah, bh, dims) + (dot(ah, bl, dims) + dot(al, bh, dims))


def summed(mask, a):
    high, rest = halves(a)
    ones = mask.astype(BF)
    return dot(ones, high, NN) + dot(ones, rest, NN)


def tie(x, *after):
    return lax.optimization_barrier((x, after))[0]


def hop(array, mask):
    count = lax.axis_size("hid")
    return lax.ppermute(array, "hid", [(i, i ^ mask) for i in range(count)])


def masks(count):
    links = [1 << b for b in range(1, count.bit_length() - 1)]
    return [1] + links, [1] + links[1:] + links[:1]


def b_offsets(count):
    _, mask_b = masks(count)
    table = np.zeros(count, np.int32)
    for t in range(count):
        for bit, mask in enumerate(mask_b):
            if t >> bit & 1:
                table[t] ^= mask
    return table


class Gather:
    def __init__(self, a, b):
        self.mask_a, self.mask_b = masks(lax.axis_size("hid"))
        self.a, self.b = a[None], b[None]

    def links(self, last, after=()):
        bits = range(1, len(self.mask_a))[-1:] if last else range(1, len(self.mask_a) - 1)
        for bit in bits:
            a, b = (tie((self.a, self.b), *after) if after else (self.a, self.b))
            got_a, got_b = hop(a, self.mask_a[bit]), hop(b, self.mask_b[bit])
            if last:
                self.late = (got_a, got_b)
            else:
                self.a = jnp.concatenate([self.a, got_a])
                self.b = jnp.concatenate([self.b, got_b])

    def early(self):
        return [self.a, self.b, hop(self.a, 1), hop(self.b, 1)]

    def latest(self, after=()):
        sent = tie(self.late, *after) if after else self.late
        return list(self.late) + [hop(x, 1) for x in sent]


class Scatter:
    def __init__(self, odd):
        self.count = lax.axis_size("hid")
        self.masks = masks(self.count)
        self.got = hop(odd, 1)

    def first(self, even):
        self.kept = [[even[ab], self.got[ab]] for ab in range(2)]
        self.bit = len(self.masks[0]) - 1
        return self.step()

    def step(self):
        half = self.kept[0][0].shape[0] // 2
        sends = [
            sum(x[half:].astype(F32) for x in kept).astype(BF) for kept in self.kept
        ]
        got = [hop(send, mask[self.bit]) for send, mask in zip(sends, self.masks)]
        self.kept = [[x[:half] for x in kept] + [g] for kept, g in zip(self.kept, got)]
        self.bit -= 1
        return sends

    def more(self):
        return self.bit >= 1

    def result(self):
        return jnp.concatenate(
            [sum(x[0].astype(F32) for x in kept) for kept in self.kept], axis=0
        )


class Sums:
    def __init__(self):
        count = lax.axis_size("seq")
        half = count // 2
        self.place = lax.axis_index("seq")
        inward = [[(i, i + 1), (count - 1 - i, count - 2 - i)] for i in range(half - 1)]
        middle = [[(half - 1, half), (half, half - 1)]]
        self.pairs = inward + middle + [[(b, a) for a, b in pair] for pair in inward[::-1]]
        self.adding = half
        self.last = [None] * len(self.pairs)
        self.flying = []
        self.count = count

    def start(self, piece, stage):
        value = piece["total"]
        if self.last[stage] is not None:
            value = tie(value, self.last[stage])
        piece["got"] = self.last[stage] = lax.ppermute(value, "seq", self.pairs[stage])
        piece["stage"] = stage

    def push(self, value):
        piece = {"total": value}
        self.start(piece, 0)
        self.flying.append(piece)
        return piece

    def tick(self, line):
        for piece in list(self.flying)[::-1]:
            self.turn(piece, line)

    def turn(self, piece, line):
        stage = piece["stage"]
        total, got = piece["total"], piece["got"]
        if stage < self.adding:
            total = line(lambda a, b: (a.astype(F32) + b.astype(F32)).astype(BF), total, got)
        else:
            (target, other) = [b for _, b in self.pairs[stage]]
            mine = (self.place == target) | (self.place == other)
            if stage + 1 < len(self.pairs):
                total = line(lambda a, b: jnp.where(mine, b, a), total, got)
            else:
                total = jnp.where(mine, got, total)
        piece["total"] = total
        if stage + 1 < len(self.pairs):
            self.start(piece, stage + 1)
        else:
            self.flying.remove(piece)

    def drain(self, line):
        while self.flying:
            self.tick(line)


class Line:
    def __init__(self):
        self.before = ()

    def __call__(self, function, *args):
        if self.before and args:
            args = tie(args, *self.before)
        result = function(*args)
        leaf = jax.tree.leaves(result)[0]
        self.before = (leaf,) if args else self.before + (leaf,)
        return result


def everywhere(value, axis):
    count = lax.axis_size(axis)
    mask = 1
    while mask < count:
        value = value + lax.ppermute(value, axis, [(i, i ^ mask) for i in range(count)])
        mask *= 2
    return value


class Entering:
    def __init__(self, state, fade, reverse):
        count = lax.axis_size("seq")
        packed = jnp.concatenate([state, jnp.repeat(fade, 16, axis=1)], axis=1).astype(BF)
        self.got = []
        for reach in range(1, count):
            step = -reach if reverse else reach
            pairs = [(i, i + step) for i in range(count) if 0 <= i + step < count]
            self.got.append(lax.ppermute(packed, "seq", pairs))

    def take(self, *got):
        border = None
        for x in got[::-1]:
            state, fade = x[:, :HDIM].astype(F32), x[:, HDIM : HDIM + 1].astype(F32)
            border = state if border is None else state + fade * border
        return border


def stream(groups, first, count, weights, outs, body, before=None):
    chips, rows, width = groups[0][0].shape
    n_sets, n_w, n_out = len(groups), len(weights), len(outs)
    n_arrays = 4 * n_sets

    def kernel(*refs):
        arrays = refs[:n_arrays]
        w_refs = refs[n_arrays : n_arrays + n_w]
        refs = refs[n_arrays + n_w + (n_out if before is not None else 0) :]
        out_refs, bufs, sem = refs[:n_out], refs[n_out:-1], refs[-1]
        i = pl.program_id(0)

        def copies(k):
            return [
                pltpu.make_async_copy(
                    arrays[4 * s + part].at[k],
                    bufs[s].at[k % 2, pl.ds(part * rows, rows)],
                    sem.at[s, k % 2, part],
                )
                for s in range(n_sets)
                for part in range(4)
            ]

        for k in range(chips):

            @pl.when(i == k)
            def _(k=k):
                if k == 0:
                    for copy in copies(0):
                        copy.start()
                if k + 1 < chips:
                    for copy in copies(k + 1):
                        copy.start()
                for copy in copies(k):
                    copy.wait()

        slot = lax.rem(i, 2)
        results = body([buf[slot] for buf in bufs], w_refs)
        for ref, value in zip(out_refs, results):
            ref[...] = value.reshape(ref.shape).astype(ref.dtype)

    anywhere = pl.BlockSpec(memory_space=pl.ANY)
    whole = lambda w: pl.BlockSpec(w.shape, lambda i: (0, 0), pipeline_mode=pl.Buffered(1))
    given = [] if before is None else list(before)
    return pl.pallas_call(
        kernel,
        grid=(chips,),
        in_specs=[anywhere] * n_arrays + [whole(w) for w in weights] + [anywhere] * len(given),
        out_specs=[
            pl.BlockSpec((2, 2, rows, c), lambda i: (i + first, 0, 0, 0)) for c, _ in outs
        ],
        out_shape=[jax.ShapeDtypeStruct((count, 2, rows, c), d) for c, d in outs],
        scratch_shapes=[pltpu.VMEM((2, 4 * rows, width), BF) for _ in groups]
        + [pltpu.SemaphoreType.DMA((n_sets, 2, 4))],
        input_output_aliases={n_arrays + n_w + o: o for o in range(len(given))},
        compiler_params=pltpu.CompilerParams(vmem_limit_bytes=VMEM),
    )(*[x for s in groups for x in s], *weights, *given)


def head_rows(rows, out_weight, count):
    own, width = rows.shape
    cols = out_weight.shape[0] // count

    def kernel(rows_ref, weight_ref, out_ref):
        out_ref[0] = dot(rows_ref[...], weight_ref[...], NT).astype(BF)

    return pl.pallas_call(
        kernel,
        grid=(count,),
        in_specs=[
            pl.BlockSpec((own, width), lambda i: (0, 0)),
            pl.BlockSpec((cols, width), lambda i: (i, 0)),
        ],
        out_specs=pl.BlockSpec((1, own, cols), lambda i: (i, 0, 0)),
        out_shape=jax.ShapeDtypeStruct((count, own, cols), BF),
        compiler_params=pltpu.CompilerParams(vmem_limit_bytes=VMEM),
    )(rows, out_weight)


def products(refs, n, dims):
    total = None
    for left, weight in zip(refs[:n], refs[n : 2 * n]):
        value = left[...]
        part = dot(value.reshape(-1, value.shape[-1]), weight[...], dims)
        total = part if total is None else total + part
    return total.astype(BF)


def partial_rows(lefts, weights, dims, parity):
    count, _, rows, _ = lefts[0].shape
    width = weights[0].shape[1 if dims == NN else 0]
    n = len(lefts)

    def kernel(*refs):
        total = products(refs, n, dims).reshape(2, 2, rows, width)
        for ab in range(2):
            refs[2 * n][ab] = total[:, ab]

    whole = lambda w: pl.BlockSpec(w.shape, lambda i: (0, 0), pipeline_mode=pl.Buffered(1))
    return pl.pallas_call(
        kernel,
        grid=(count // 4,),
        in_specs=[
            pl.BlockSpec((2, 1, 2, rows, x.shape[-1]), lambda i: (i, parity, 0, 0, 0))
            for x in lefts
        ]
        + [whole(w) for w in weights],
        out_specs=pl.BlockSpec((2, 2, rows, width), lambda i: (0, i, 0, 0)),
        out_shape=jax.ShapeDtypeStruct((2, count // 2, rows, width), BF),
        compiler_params=pltpu.CompilerParams(vmem_limit_bytes=VMEM),
    )(*[x.reshape((count // 2, 2) + x.shape[1:]) for x in lefts], *weights)


def owned_rows(lefts, weights, dims, table):
    count, _, rows, _ = lefts[0].shape
    width = weights[0].shape[1 if dims == NN else 0]
    n = len(lefts)

    def kernel(tab, *refs):
        i = pl.program_id(0)
        total = products(refs, n, dims).reshape(2, 2, rows, width)
        for c in range(2):
            for ab in range(2):
                refs[2 * n][tab[ab * count + 2 * i + c], ab] = total[c, ab]

    return pl.pallas_call(
        kernel,
        grid_spec=pltpu.PrefetchScalarGridSpec(
            num_scalar_prefetch=1,
            grid=(count // 2,),
            in_specs=[
                pl.BlockSpec((2, 2, rows, x.shape[-1]), lambda i, tab: (i, 0, 0, 0))
                for x in lefts
            ]
            + [
                pl.BlockSpec(w.shape, lambda i, tab: (0, 0), pipeline_mode=pl.Buffered(1))
                for w in weights
            ],
            out_specs=pl.BlockSpec((count, 2, rows, width), lambda i, tab: (0, 0, 0, 0)),
        ),
        out_shape=jax.ShapeDtypeStruct((count, 2, rows, width), BF),
        compiler_params=pltpu.CompilerParams(vmem_limit_bytes=VMEM),
    )(table, *lefts, *weights)


def outer_rows(moved, rows, table):
    count, own, cols = moved.shape
    width = rows.shape[1]
    half = cols // 2

    def kernel(tab, a_ref, b_ref, rows_ref, out_ref):
        value = rows_ref[...]
        for ab, ref in enumerate((a_ref, b_ref)):
            left = ref[0].astype(F32).T[ab * half : (ab + 1) * half].astype(BF)
            out_ref[0, ab, 0] = dot(left, value, NN).astype(BF)

    return pl.pallas_call(
        kernel,
        grid_spec=pltpu.PrefetchScalarGridSpec(
            num_scalar_prefetch=1,
            grid=(count,),
            in_specs=[
                pl.BlockSpec((1, own, cols), lambda t, tab: (tab[t], 0, 0)),
                pl.BlockSpec((1, own, cols), lambda t, tab: (tab[count + t], 0, 0)),
                pl.BlockSpec((own, width), lambda t, tab: (0, 0)),
            ],
            out_specs=pl.BlockSpec(
                (1, 2, 1, half, width), lambda t, tab: (t % 2, 0, t // 2, 0, 0)
            ),
        ),
        out_shape=jax.ShapeDtypeStruct((2, 2, count // 2, half, width), BF),
        compiler_params=pltpu.CompilerParams(vmem_limit_bytes=VMEM),
    )(table, moved, moved, rows)


def attend(moved, out_weight, own_rows, gain):
    count, rows, cols = moved.shape
    depth, width = out_weight.shape
    block = 512
    steps = width // block

    def kernel(moved_ref, weight_ref, own_ref, gain_ref, res_ref, normed_ref, left_ref):
        i = pl.program_id(0)

        @pl.when(i == 0)
        def _():
            for s in range(count):
                left_ref[:, s * cols : (s + 1) * cols] = moved_ref[s]

        part = dot(left_ref[...], weight_ref[...], NN)
        for k in range(steps):

            @pl.when(i == k)
            def _(k=k):
                at = slice(k * block, (k + 1) * block)
                res_ref[:, at] = own_ref[:, at].astype(F32) + part

        @pl.when(i == steps - 1)
        def _():
            value = res_ref[...]
            scale = lax.rsqrt(jnp.mean(value * value, axis=-1, keepdims=True) + 1e-06)
            normed_ref[...] = (value * scale * gain_ref[...]).astype(BF)

    return pl.pallas_call(
        kernel,
        grid=(steps,),
        in_specs=[
            pl.BlockSpec((count, rows, cols), lambda i: (0, 0, 0)),
            pl.BlockSpec((depth, block), lambda i: (0, i)),
            pl.BlockSpec((rows, width), lambda i: (0, 0)),
            pl.BlockSpec((1, width), lambda i: (0, 0)),
        ],
        out_specs=[pl.BlockSpec((rows, width), lambda i: (0, 0))] * 2,
        out_shape=[
            jax.ShapeDtypeStruct((rows, width), F32),
            jax.ShapeDtypeStruct((rows, width), BF),
        ],
        scratch_shapes=[pltpu.VMEM((rows, depth), BF)],
        compiler_params=pltpu.CompilerParams(vmem_limit_bytes=VMEM),
    )(moved, out_weight, own_rows, gain)


class Scan:
    def __init__(self, count, seqs, rows, cols, table, base, lengths, lower):
        self.count, self.rows, self.cols = count, rows, cols
        self.per = seqs // 2
        self.heads = cols // HDIM
        self.total = seqs * self.heads
        self.scalars = jnp.concatenate([table, base[None], lengths]).astype(jnp.int32)
        self.lower = lower.reshape(1, cols)

    def slots(self, part, width, reverse):
        n = self.count

        def of(ab):
            def place(p, sc):
                p = n - 1 - p if reverse else p
                return (sc[ab * n + p], ab, 0, part)

            return pl.BlockSpec((1, 1, self.per * self.rows, width), place)

        return [of(0), of(1)]

    def chunk(self, shape, reverse):
        n = self.count
        zeros = (0,) * (len(shape) - 1)
        return pl.BlockSpec(
            (1,) + tuple(shape[1:]), lambda p, sc: ((n - 1 - p if reverse else p),) + zeros
        )

    def whole(self, shape):
        zeros = (0,) * len(shape)
        return pl.BlockSpec(tuple(shape), lambda p, sc: zeros)

    def call(self, kernel, in_specs, out_specs, out_shape, scratch, args):
        return pl.pallas_call(
            kernel,
            grid_spec=pltpu.PrefetchScalarGridSpec(
                num_scalar_prefetch=1,
                grid=(self.count,),
                in_specs=in_specs,
                out_specs=out_specs,
                scratch_shapes=scratch,
            ),
            out_shape=out_shape,
            compiler_params=pltpu.CompilerParams(vmem_limit_bytes=VMEM),
        )(self.scalars, *args)

    def units(self):
        for ab in range(2):
            for s in range(self.per):
                yield ab, s, slice(s * self.rows, (s + 1) * self.rows)

    def state(self, ab, s, h):
        return (ab * self.per + s) * self.heads + h

    def valid(self, sc, p, ab, s):
        n = self.count
        pos = sc[2 * n] + p * self.rows + lax.broadcasted_iota(jnp.int32, (self.rows, 1), 0)
        return (pos < sc[2 * n + 1 + ab * self.per + s]).astype(F32)

    def triangle(self):
        r = lax.broadcasted_iota(jnp.int32, (self.rows, self.rows), 0)
        c = lax.broadcasted_iota(jnp.int32, (self.rows, self.rows), 1)
        return r >= c, r <= c

    def rates(self, forget, lower, valid):
        negative = jax.nn.sigmoid(-forget)
        keys = valid * (1.0 - lower) * negative
        down, _ = self.triangle()
        cum = summed(down.astype(F32), jnp.log(1.0 - keys))
        return negative, keys, cum

    def ends(self, joint):
        n, total, c = self.count, self.total, self.cols

        def kernel(sc, fa_ref, fb_ref, va_ref, vb_ref, lower_ref, end_ref, fade_ref, sum_ref):
            p = pl.program_id(0)

            @pl.when(p == 0)
            def _():
                end_ref[...] = jnp.zeros(end_ref.shape, F32)
                fade_ref[...] = jnp.ones(fade_ref.shape, F32)
                sum_ref[...] = jnp.zeros(sum_ref.shape, F32)

            gates = jnp.zeros((1, c), F32)
            for ab, s, sp in self.units():
                f_ref, v_ref = (fa_ref, fb_ref)[ab], (va_ref, vb_ref)[ab]
                valid = self.valid(sc, p, ab, s)
                _, keys, cum = self.rates(f_ref[0, 0, sp], lower_ref[...], valid)
                last = cum[self.rows - 1 :]
                gates += jnp.sum(valid * (1.0 - keys), axis=0, keepdims=True)
                to_end = keys * jnp.exp(last - cum)
                fade = jnp.exp(last)
                values = v_ref[0, 0, sp]
                for h in range(self.heads):
                    at = self.state(ab, s, h)
                    ch = slice(h * HDIM, (h + 1) * HDIM)
                    grown = dot3(values[:, ch], to_end[:, ch], TN)
                    end_ref[at] = end_ref[at] * fade[:, ch] + grown
                    fade_ref[at] = fade_ref[at] * fade[:, ch]
            sum_ref[...] += gates

        shapes = [
            jax.ShapeDtypeStruct((total, HDIM, HDIM), F32),
            jax.ShapeDtypeStruct((total, 1, HDIM), F32),
            jax.ShapeDtypeStruct((1, c), F32),
        ]
        return self.call(
            kernel,
            self.slots(1, c, False) + self.slots(2, c, False) + [self.whole((1, c))],
            [self.whole(x.shape) for x in shapes],
            shapes,
            [],
            (joint,) * 4 + (self.lower,),
        )

    def forward(self, joint):
        n, total, c = self.count, self.total, self.cols
        rows = self.per * self.rows

        def kernel(sc, ja_ref, jb_ref, lower_ref, mix_ref, reach_ref, start_ref, fade_ref, state_ref, kept_ref):
            p = pl.program_id(0)

            @pl.when(p == 0)
            def _():
                state_ref[...] = jnp.zeros(state_ref.shape, F32)
                kept_ref[...] = jnp.ones(kept_ref.shape, F32)

            down, _ = self.triangle()
            mid_row = self.rows // 2 - 1
            for ab, s, sp in self.units():
                joint_ref = (ja_ref, jb_ref)[ab]
                valid = self.valid(sc, p, ab, s)
                queries = joint_ref[0, 0, sp, 0:c]
                values = joint_ref[0, 0, sp, 2 * c : 3 * c]
                _, keys, cum = self.rates(joint_ref[0, 0, sp, c : 2 * c], lower_ref[...], valid)
                mid, last = cum[mid_row : mid_row + 1], cum[self.rows - 1 :]
                q_mid = queries * jnp.exp(cum - mid)
                k_mid = keys * jnp.exp(mid - cum)
                q_start = q_mid * jnp.exp(mid)
                to_end = k_mid * jnp.exp(last - mid)
                fade = jnp.exp(last)
                for h in range(self.heads):
                    at = self.state(ab, s, h)
                    ch = slice(h * HDIM, (h + 1) * HDIM)
                    state, kept = state_ref[at], kept_ref[at]
                    start_ref[0, at] = state
                    fade_ref[0, at] = kept
                    scores = jnp.where(down, dot3(q_mid[:, ch], k_mid[:, ch], NT), 0.0)
                    mix = dot3(scores, values[:, ch], NN) + dot3(q_start[:, ch], state, NT)
                    state_ref[at] = state * fade[:, ch] + dot3(values[:, ch], to_end[:, ch], TN)
                    mix_ref[0, ab, sp, ch] = mix
                    reach_ref[0, ab, sp, ch] = q_start[:, ch] * kept
                    kept_ref[at] = kept * fade[:, ch]

        shapes = [
            jax.ShapeDtypeStruct((n, 2, rows, c), F32),
            jax.ShapeDtypeStruct((n, 2, rows, c), F32),
            jax.ShapeDtypeStruct((n, total, HDIM, HDIM), F32),
            jax.ShapeDtypeStruct((n, total, 1, HDIM), F32),
        ]
        return self.call(
            kernel,
            self.slots(0, 4 * c, False) + [self.whole((1, c))],
            [self.chunk(x.shape, False) for x in shapes],
            shapes,
            [pltpu.VMEM((total, HDIM, HDIM), F32), pltpu.VMEM((total, 1, HDIM), F32)],
            (joint, joint, self.lower),
        )

    def finish(self, joint, mixture, reach, initial, head_gain):
        n, total, c = self.count, self.total, self.cols
        rows = self.per * self.rows

        def kernel(sc, ga_ref, gb_ref, local_ref, reach_ref, init_ref, gain_ref, mix_ref, out_ref):
            p = pl.program_id(0)
            for ab, s, sp in self.units():
                gates = (ga_ref, gb_ref)[ab][0, 0, sp]
                valid = self.valid(sc, p, ab, s)
                scale = gain_ref[...] * (gates * jax.nn.sigmoid(gates)) * valid
                for h in range(self.heads):
                    at = self.state(ab, s, h)
                    ch = slice(h * HDIM, (h + 1) * HDIM)
                    mix = local_ref[0, ab, sp, ch] + dot3(reach_ref[0, ab, sp, ch], init_ref[at], NT)
                    rho = lax.rsqrt(jnp.mean(mix * mix, axis=-1, keepdims=True) + 1e-05)
                    mix_ref[0, ab, sp, ch] = mix
                    out_ref[0, ab, sp, ch] = (mix * rho * scale[:, ch]).astype(BF)

        shapes = [
            jax.ShapeDtypeStruct((n, 2, rows, c), F32),
            jax.ShapeDtypeStruct((n, 2, rows, c), BF),
        ]
        chunk = self.chunk(mixture.shape, False)
        return self.call(
            kernel,
            self.slots(3, c, False)
            + [chunk, chunk, self.whole((total, HDIM, HDIM)), self.whole((1, c))],
            [chunk, chunk],
            shapes,
            [],
            (joint, joint, mixture, reach, initial, head_gain.reshape(1, c)),
        )

    def finish_back(self, joint, mixture, grad_gated, head_gain):
        n, total, c = self.count, self.total, self.cols
        rows = self.per * self.rows

        def kernel(
            sc, qa_ref, qb_ref, fa_ref, fb_ref, ga_ref, gb_ref, mix_ref, grad_ref,
            lower_ref, gain_ref, gm_ref, gate_ref, head_ref, reach_ref,
        ):
            step = pl.program_id(0)
            p = n - 1 - step

            @pl.when(step == 0)
            def _():
                head_ref[...] = jnp.zeros(head_ref.shape, F32)
                reach_ref[...] = jnp.zeros(reach_ref.shape, F32)

            gain = gain_ref[...]
            heads = [jnp.zeros((1, HDIM), F32)] * self.heads
            for ab, s, sp in self.units():
                q_ref, f_ref, g_ref = (qa_ref, qb_ref)[ab], (fa_ref, fb_ref)[ab], (ga_ref, gb_ref)[ab]
                slot = sc[ab * n + p]
                valid = self.valid(sc, p, ab, s)
                _, _, cum = self.rates(f_ref[0, 0, sp], lower_ref[...], valid)
                q_start = q_ref[0, 0, sp] * jnp.exp(cum)
                fade = jnp.exp(cum[self.rows - 1 :])
                gates = g_ref[0, 0, sp]
                sig = jax.nn.sigmoid(gates)
                arriving = grad_ref[0, ab, sp].astype(F32) * valid
                e = arriving * (gates * sig)
                slope = arriving * gain * sig * (1.0 + gates * (1.0 - sig))
                for h in range(self.heads):
                    at = self.state(ab, s, h)
                    ch = slice(h * HDIM, (h + 1) * HDIM)
                    mix = mix_ref[0, ab, sp, ch]
                    rho = lax.rsqrt(jnp.mean(mix * mix, axis=-1, keepdims=True) + 1e-05)
                    scaled = mix * rho
                    heads[h] += jnp.sum(e[:, ch] * scaled, axis=0, keepdims=True)
                    ge = gain[:, ch] * e[:, ch]
                    gm = rho * ge - mix * (rho * rho * rho) * jnp.mean(
                        mix * ge, axis=-1, keepdims=True
                    )
                    gm_ref[0, ab, sp, ch] = gm
                    gate_ref[slot, ab, sp, ch] = (scaled * slope[:, ch]).astype(BF)
                    reach_ref[at] = reach_ref[at] * fade[:, ch] + dot3(gm, q_start[:, ch], TN)
            for h in range(self.heads):
                head_ref[:, h * HDIM : (h + 1) * HDIM] += heads[h]

        shapes = [
            jax.ShapeDtypeStruct((n, 2, rows, c), F32),
            jax.ShapeDtypeStruct((n, 2, rows, c), BF),
            jax.ShapeDtypeStruct((1, c), F32),
            jax.ShapeDtypeStruct((total, HDIM, HDIM), F32),
        ]
        slots = lambda part: self.slots(part, c, True)
        return self.call(
            kernel,
            slots(0) + slots(1) + slots(3)
            + [self.chunk(mixture.shape, True), self.chunk(mixture.shape, True)]
            + [self.whole((1, c)), self.whole((1, c))],
            [self.chunk(shapes[0].shape, True)] + [self.whole(x.shape) for x in shapes[1:]],
            shapes,
            [],
            (joint,) * 6 + (mixture, grad_gated, self.lower, head_gain.reshape(1, c)),
        )

    def backward(self, joint, grad_mix, starts, fades, initial, final, leaving):
        n, total, c = self.count, self.total, self.cols
        rows = self.per * self.rows

        def kernel(
            sc, qa_ref, qb_ref, fa_ref, fb_ref, va_ref, vb_ref, gm_ref, start_ref, fade_ref,
            init_ref, final_ref, leave_ref, lower_ref, out_ref, low_ref, back_ref, end_ref,
        ):
            step = pl.program_id(0)
            p = n - 1 - step

            @pl.when(step == 0)
            def _():
                back_ref[...] = leave_ref[...]
                end_ref[...] = final_ref[...]
                low_ref[...] = jnp.zeros(low_ref.shape, F32)

            down, up = self.triangle()
            mid_row = self.rows // 2 - 1
            room = 1.0 - lower_ref[...]
            lows = [jnp.zeros((1, HDIM), F32)] * self.heads
            for ab, s, sp in self.units():
                q_ref, f_ref, v_ref = (qa_ref, qb_ref)[ab], (fa_ref, fb_ref)[ab], (va_ref, vb_ref)[ab]
                slot = sc[ab * n + p]
                valid = self.valid(sc, p, ab, s)
                queries, values = q_ref[0, 0, sp], v_ref[0, 0, sp]
                forget = f_ref[0, 0, sp]
                neg, keys, cum = self.rates(forget, lower_ref[...], valid)
                mid, last = cum[mid_row : mid_row + 1], cum[self.rows - 1 :]
                from_mid, to_mid = jnp.exp(cum - mid), jnp.exp(mid - cum)
                start_mid, mid_last = jnp.exp(mid), jnp.exp(last - mid)
                q_mid, k_mid = queries * from_mid, keys * to_mid
                q_start, k_last = q_mid * start_mid, k_mid * mid_last
                fade = jnp.exp(last)
                pos = jax.nn.sigmoid(forget)
                for h in range(self.heads):
                    at = self.state(ab, s, h)
                    ch = slice(h * HDIM, (h + 1) * HDIM)
                    gm, val = gm_ref[0, ab, sp, ch], values[:, ch]
                    start, back = start_ref[0, at] + fade_ref[0, at] * init_ref[at], back_ref[at]
                    scores = jnp.where(down, dot3(q_mid[:, ch], k_mid[:, ch], NT), 0.0)
                    pull = jnp.where(down, dot3(gm, val, NT), 0.0)
                    gq = from_mid[:, ch] * (
                        dot3(pull, k_mid[:, ch], NN) + dot3(gm, start, NN) * start_mid[:, ch]
                    )
                    gv = dot3(scores, gm, TN) + dot3(k_last[:, ch], back, NT)
                    gk = to_mid[:, ch] * (
                        dot3(pull, q_mid[:, ch], TN) + dot3(val, back, NN) * mid_last[:, ch]
                    )
                    at_end = jnp.sum(back * end_ref[at], axis=0, keepdims=True)
                    fading = at_end + summed(
                        up.astype(F32), queries[:, ch] * gq - keys[:, ch] * gk
                    )
                    gk = gk - fading / (1.0 - keys[:, ch])
                    gk_valid = gk * valid * neg[:, ch]
                    lows[h] += jnp.sum(gk_valid, axis=0, keepdims=True)
                    gf = -gk_valid * room[:, ch] * pos[:, ch]
                    for part, value in enumerate((gq, gf, gv)):
                        at_col = part * c + h * HDIM
                        out_ref[slot, ab, sp, at_col : at_col + HDIM] = value.astype(BF)
                    end_ref[at] = start
                    back_ref[at] = back * fade[:, ch] + dot3(gm, q_start[:, ch], TN)
            for h in range(self.heads):
                low_ref[:, h * HDIM : (h + 1) * HDIM] -= lows[h]

        shapes = [
            jax.ShapeDtypeStruct((n, 2, rows, 3 * c), BF),
            jax.ShapeDtypeStruct((1, c), F32),
        ]
        slots = lambda part: self.slots(part, c, True)
        states = self.whole((total, HDIM, HDIM))
        return self.call(
            kernel,
            slots(0) + slots(1) + slots(2)
            + [self.chunk(grad_mix.shape, True), self.chunk(starts.shape, True), self.chunk(fades.shape, True)]
            + [states] * 3
            + [self.whole((1, c))],
            [self.whole(x.shape) for x in shapes],
            shapes,
            [pltpu.VMEM((total, HDIM, HDIM), F32)] * 2,
            (joint,) * 6 + (grad_mix, starts, fades, initial, final, leaving, self.lower),
        )


def norm_back(values, gain, grad, epsilon):
    scale = lax.rsqrt(jnp.mean(values * values, axis=-1, keepdims=True) + epsilon)
    pulled = gain * grad
    grad_values = scale * pulled - values * (scale * scale * scale) * jnp.mean(
        values * pulled, axis=-1, keepdims=True
    )
    return grad_values, jnp.sum(values * scale * grad, axis=0)


def weight_grad(left, right):
    return lax.dot_general(left, right, TN, preferred_element_type=F32).astype(BF)


def shards(
    tokens,
    lengths,
    cotangent,
    mixer_gain,
    query_weight,
    forget_weight,
    input_weight,
    gate_weight,
    lower_bound,
    head_gain,
    out_weight,
    feed_gain,
    feed_gate_weight,
    up_weight,
    down_weight,
):
    count = lax.axis_size("hid")
    me = lax.axis_index("hid")
    rows, seqs, width = tokens.shape
    cols = query_weight.shape[1]
    units = feed_gate_weight.shape[1]
    base = lax.axis_index("seq") * (rows * count)
    own = seqs * rows
    cut = own // 2

    def halves_of(array):
        return array[:cut], array[cut:]

    def to_rows(array):
        return jnp.transpose(array, (1, 0, 2)).reshape(own, width)

    def from_rows(array):
        return jnp.transpose(array.reshape(seqs, rows, width), (1, 0, 2))

    flat = lambda x: x.reshape(-1, x.shape[-1])
    offsets = jnp.concatenate([jnp.arange(count), jnp.asarray(b_offsets(count))]) ^ me
    inverse = np.argsort(b_offsets(count)).astype(np.int32)
    places = jnp.arange(count) ^ me
    table = jnp.concatenate([places, jnp.asarray(inverse)[places]])
    scan = Scan(count, seqs, rows, cols, table, base, lengths, lower_bound)
    line = Line()
    gate_t, up_t = feed_gate_weight.T, up_weight.T

    own_rows = to_rows(tokens)
    inputs = own_rows.astype(F32)
    in_scale = lax.rsqrt(jnp.mean(inputs * inputs, axis=-1, keepdims=True) + 1e-06)
    normed_in = (inputs * in_scale * mixer_gain).astype(BF)
    going = Gather(*halves_of(normed_in))
    going.links(False)
    going.links(True)
    joint_weights = (query_weight, forget_weight, input_weight, gate_weight)
    joint_out = [(4 * cols, F32), (width, BF)]

    def project(group, first, before=None):
        def body(xs, w_refs):
            return [jnp.concatenate([dot(xs[0], w[...], NN) for w in w_refs], axis=1), xs[0]]

        return line(
            lambda group, before: stream(
                [group], first, count, joint_weights, joint_out, body, before
            ),
            group,
            before,
        )

    part = project(going.early(), 0)
    cot_rows = tie(to_rows(cotangent), part[0])
    latest = going.latest((part[0], cot_rows))
    cots = Gather(*tie(halves_of(cot_rows), latest))
    cots.links(False)
    joint, in_rows = project(latest, count // 4, part)
    ends, fade, gate_sums = line(scan.ends, joint)
    entry = Entering(ends, fade, False)
    cots.links(True, (ends,))
    mixture, reach, starts, fades = line(scan.forward, joint)
    initial = line(entry.take, *entry.got)
    mixture, gated_p = line(scan.finish, joint, mixture, reach, initial, head_gain)
    moved = lax.all_to_all(
        gated_p.reshape(count, own, cols), "hid", split_axis=0, concat_axis=0, tiled=True
    )
    cot_early = tie((cots.a, cots.b), gated_p)
    cot_early = list(cot_early) + [hop(x, 1) for x in cot_early]
    cot_latest = cots.latest((gated_p,))
    residual, normed_feed = line(
        lambda m, _: attend(m, out_weight, own_rows, feed_gain.reshape(1, width)),
        moved,
        (cot_early, cot_latest),
    )

    going = Gather(*halves_of(normed_feed))
    going.links(False)
    going.links(True)
    feed_weights = (gate_t, up_t, down_weight)
    feed_shapes = [(units, BF)] * 3 + [(width, BF)] * 2

    def feed(group, cot_group, first, before=None):
        def body(xs, w_refs):
            gate = dot(xs[0], w_refs[0][...], NT)
            up = dot(xs[0], w_refs[1][...], NT)
            grad_hidden = dot(xs[1], w_refs[2][...], NT)
            sig = jax.nn.sigmoid(gate)
            silu = gate * sig
            grad_gate = grad_hidden * up * sig * (1.0 + gate * (1.0 - sig))
            return [silu * up, grad_gate, grad_hidden * silu, xs[0], xs[1]]

        return line(
            lambda group, cot_group, before: stream(
                [group, cot_group], first, count, feed_weights, feed_shapes, body, before
            ),
            group,
            cot_group,
            before,
        )

    part = feed(going.early(), cot_early, 0)
    hidden, grad_feed_gate, grad_up, feed_rows, grad_rows = feed(
        going.latest((part[0],)), cot_latest, count // 4, part
    )
    hidden_f, gate_f, up_f = flat(hidden), flat(grad_feed_gate), flat(grad_up)
    feed_f, grad_f = flat(feed_rows), flat(grad_rows)
    spread = lambda x: lax.psum_scatter(
        x.reshape(-1, width), "hid", scatter_dimension=0, tiled=True
    )
    down_w = line(weight_grad, hidden_f, grad_f)
    gate_w = line(weight_grad, gate_f, feed_f)
    up_w = line(weight_grad, up_f, feed_f)
    down_w, gate_w, up_w = lax.psum((down_w, gate_w, up_w), "seq")
    backs = lambda parity: line(
        lambda *a: partial_rows(a, (gate_t, up_t), NN, parity), grad_feed_gate, grad_up
    )
    shrink = Scatter(backs(1))
    even = backs(0)
    line(shrink.first, even)
    while shrink.more():
        line(lambda: shrink.step())

    def after_feed(grad):
        cot = to_rows(cotangent).astype(F32)
        grad_part, grad_gain = norm_back(residual, feed_gain, grad, 1e-06)
        grad_residual = cot + grad_part
        return grad_residual.astype(BF), grad_residual, grad_gain

    grad_attended, grad_residual, grad_feed_gain = line(after_feed, shrink.result())

    sent = line(lambda rows: head_rows(rows, out_weight, count), grad_attended)
    grad_gated = lax.all_to_all(sent, "hid", split_axis=0, concat_axis=0, tiled=True)
    feed_out = line(lambda *a: owned_rows(a, (down_weight,), NN, offsets), hidden)
    feed_out = spread(feed_out)
    grad_mix, grad_gate, grad_head, reach = line(
        scan.finish_back, joint, mixture, grad_gated.reshape(mixture.shape), head_gain
    )
    leave = Entering(reach, fade, True)
    in_f = flat(in_rows)
    mix_gate = line(weight_grad, in_f, flat(grad_gate))
    out_full = line(lambda m, g: outer_rows(m, g, offsets), moved, grad_attended)
    narrow = Scatter(out_full[1])
    leaving = line(leave.take, *leave.got)
    line(narrow.first, out_full[0])
    final = ends + fade * initial
    sums = Sums()
    mix_gate = sums.push(tie(mix_gate, leaving))
    grad_three, grad_lower = line(
        scan.backward, joint, grad_mix, starts, fades, initial, final, leaving
    )
    while narrow.more():
        line(lambda: narrow.step())
    three_w = line(weight_grad, in_f, flat(grad_three))
    quarter = width // 4
    threes = [three_w[i * quarter : (i + 1) * quarter] for i in range(4)]
    out_part = line(lambda x: x.astype(BF), narrow.result())
    sums.tick(line)
    out_part = sums.push(out_part)
    joint_three = jnp.concatenate(joint_weights[:3], axis=1)
    backs = lambda parity: line(
        lambda *a: partial_rows(a, (joint_three, gate_weight), NT, parity), grad_three, grad_gate
    )
    shrink = Scatter(backs(1))
    even = backs(0)
    sums.tick(line)
    threes[0] = sums.push(threes[0])
    line(shrink.first, even)
    sums.tick(line)
    threes[1] = sums.push(threes[1])
    while shrink.more():
        line(lambda: shrink.step())
    sums.tick(line)
    threes[2] = sums.push(threes[2])
    grad_in, grad_mixer = line(lambda g: norm_back(inputs, mixer_gain, g, 1e-06), shrink.result())
    small = everywhere(
        jnp.concatenate([grad_mixer, grad_feed_gain, jnp.sum(gate_sums).reshape(1)]), "hid"
    )
    grad_tokens = line(lambda a, b: from_rows(a + b), grad_residual, grad_in)
    sums.tick(line)
    threes[3] = sums.push(threes[3])
    small = everywhere(jnp.concatenate([small, grad_lower[0], grad_head[0]]), "seq")
    heads = small[2 * width + 1 :]
    down_w, gate_w, up_w = line(
        lambda d, *x: (d.astype(F32), *[y.astype(F32).T for y in x]), down_w, gate_w, up_w
    )
    gathered_out = lax.all_gather(out_part["total"], "hid", axis=0, tiled=True)
    output = line(lambda a, b: from_rows((a + b).astype(BF)), residual, feed_out)
    sums.tick(line)
    grad_out = line(lambda x: x.astype(F32), gathered_out)
    sums.drain(line)
    total = lambda *parts: jnp.concatenate([p["total"] for p in parts], axis=0).astype(F32)
    three_w = total(*threes)
    mean_forget = small[2 * width] / (width * jnp.sum(lengths).astype(F32))
    return (
        output,
        grad_tokens,
        small[:width],
        three_w[:, :cols],
        three_w[:, cols : 2 * cols],
        three_w[:, 2 * cols :],
        total(mix_gate),
        heads[:cols],
        heads[cols:],
        grad_out,
        small[width : 2 * width],
        gate_w,
        up_w,
        down_w,
        mean_forget,
    )


def solution(mesh):
    rows = P(("seq", "hid"), None, None)
    columns = P(None, "hid")
    return jax.shard_map(
        shards,
        mesh=mesh,
        in_specs=(
            rows,
            P(),
            rows,
            P(),
            columns,
            columns,
            columns,
            columns,
            P("hid"),
            P("hid"),
            P(),
            P(),
            columns,
            columns,
            P("hid", None),
        ),
        out_specs=(
            rows,
            rows,
            P(),
            columns,
            columns,
            columns,
            columns,
            P("hid"),
            P("hid"),
            P(),
            P(),
            columns,
            columns,
            P("hid", None),
            P(),
        ),
        check_vma=False,
    )
```
